32 devices in a mesh: req: 4 (over z), ep: 8 (over y, x, core).
Axes of the slice: x: 2, y: 2, z: 4, core: 2. Of those that a mesh axis runs over, the one named last changes fastest.
Arguments:
- query: bfloat16 [128, 2, 4096], P('req', None, 'ep'), may hold values from -6 to 6
- key_in: bfloat16 [128, 2, 4096], P('req', None, 'ep'), may hold values from -6 to 6
- value: bfloat16 [128, 2, 4096], P('req', None, 'ep'), may hold values from -6 to 6
- gate_z: bfloat16 [128, 2, 4096], P('req', None, 'ep'), may hold values from -6 to 6
- alpha_in: float32 [128, 2, 32], P('req', None, 'ep'), may hold values from -6 to 6
- beta_in: float32 [128, 2, 32], P('req', None, 'ep'), may hold values from -9 to 9
- a_log: float32 [32], P('ep'), may hold values from -2 to 0.5
- dt_bias: float32 [32], P('ep'), may hold values from -1 to 1
- norm_gain: float32 [128], replicated, may hold values from 0.5 to 1.5
- state: bfloat16 [128, 32, 128, 128], P('req', 'ep'), may hold values from -6 to 6
- out_weight: bfloat16 [4096, 2048], P('ep'), may hold values from -0.125 to 0.125
- hidden: bfloat16 [128, 2, 2048], P('req'), may hold values from -6 to 6
- post_gain: float32 [2048], replicated, may hold values from 0.5 to 1.5
- expert_in: bfloat16 [512, 2048, 512], P(('req', 'ep')), may hold values from -0.125 to 0.125
- expert_out: bfloat16 [512, 256, 2048], P(('req', 'ep')), may hold values from -0.25 to 0.25
- expert_ids: int32 [128, 2, 10], P('req'), may hold values from 0 to 255, all different within a row; in each aligned block of 64 rows (0 to 63, 64 to 127, ..., all dimensions but the last counted through in order) at most 4 rows name the same one
- route_weights: bfloat16 [128, 2, 10], P('req'), may hold values from 0.049804688 to 0.29882812
Outputs:
- mixed: bfloat16 [128, 2, 2048], P('req', None, 'ep')
The draws below stay inside these ranges and needn't reach their ends.
Inputs may be any that keep to these rules, and one draw needn't show every extreme that they name: `expert_ids`: within the rows of one index of req (32 requests, 2 positions each) no expert is named by more than 4 rows, a bound that some block reaches of them. The 10 experts of a row differ.
All inputs are finite; a program needn't handle non-finite values.
Results may differ from the reference program's by a relative error of at most 0.012.
Values may be sent and summed in bfloat16 or wider, within the bound.
A program may use at most 128 MiB of HBM per device.

```python
import math
import jax
import jax.numpy as jnp
import numpy as np
from jax import lax

D = 2048
HEADS = 32
DK = 128
DV = 128
HALF = 256
EXPERTS = 256
TOPK = 10
MOST = 4
STEPS = 2
R_DEV = 32
REQS = 128
N_REQ = 4


def strengthened(values, rng, source, target, parts, factor):
    def block_of(dim):
        return (jnp.arange(values.shape[dim]) // (values.shape[dim] // parts)).reshape((-1,) + (1,) * (values.ndim - 1 - dim))

    near = jax.random.permutation(rng, parts)[block_of(target)]
    far = (block_of(target) + parts // 2) % parts
    return jnp.where((block_of(source) == near) | (block_of(source) == far), factor * values, values)


def block_levels(stream_key, dims, pieces, low, high):
    factor_of, own = 1.0, jax.random.fold_in(stream_key, 6)
    for axis_at, blocks in pieces:
        steps = jnp.exp(jax.random.uniform(jax.random.fold_in(own, axis_at), (blocks,), jnp.float32, low / len(pieces), high / len(pieces)))
        factor_of = factor_of * jnp.repeat(steps, dims[axis_at] // blocks).reshape([-1 if axis == axis_at else 1 for axis in range(len(dims))])
    return factor_of


def routed_block(own_key, own, number, rows, number_of, top, most, lean):
    order = jax.random.permutation(own_key, number_of)
    crowded, ordinary = portions_of(number_of, rows * top, most, lean, True), portions_of(number_of, rows * top, most, lean, False)
    places = jnp.arange(number_of)

    def named(tallies, turn):
        used = int((tallies > 0).sum())
        fixed = max(1, used // 4)
        shifted = fixed + (places - fixed + turn * (used - fixed)) % max(1, number_of - fixed)
        return jnp.zeros((number_of,), jnp.int32).at[order[jnp.where(places < fixed, places, shifted)]].set(jnp.asarray(tallies, jnp.int32))

    tallies = jnp.where(number % 4 == 0, named(crowded, number // 4), named(ordinary, number - number // 4 - 1))
    mixed = jax.random.permutation(jax.random.fold_in(own, 3), number_of)
    giver, sink = mixed[0:number_of // 2 * 2:2], mixed[1:number_of // 2 * 2:2]
    room = jnp.minimum(tallies[giver] - 1, most - tallies[sink]) // 2
    room = jnp.where((giver == order[0]) | (sink == order[0]) | (tallies[sink] == 0), 0, jnp.maximum(room, 0))
    shifted = jax.random.randint(jax.random.fold_in(own, 4), (number_of // 2,), 0, 1 << 20) % (room + 1)
    tallies = tallies.at[giver].add(-shifted).at[sink].add(shifted)
    members = jnp.searchsorted(jnp.cumsum(tallies), jnp.arange(rows * top), side="right").astype(jnp.int32)
    listing = members.reshape(top, rows).T
    listing = listing[jax.random.permutation(jax.random.fold_in(own, 1), rows)]
    turn = jax.random.randint(jax.random.fold_in(own, 2), (rows, 1), 0, top)
    return jnp.take_along_axis(listing, (jnp.arange(top)[None, :] + turn) % top, axis=1)


def portions_of(amount, total, limit, skew, full):
    portions = [(1 << 20) // math.isqrt(rank ** skew) + 1 for rank in range(1, amount + 1)]
    largest = limit if full else min(limit, max(-(-total // amount), total * portions[0] // sum(portions)))
    least = 1 if total - largest >= amount - 1 else 0
    counts, spare = [largest] + [least] * (amount - 1), total - largest - least * (amount - 1)
    while spare > 0:
        candidates = [i for i in range(1, amount) if counts[i] < largest] or [i for i in range(1, amount) if counts[i] < limit]
        pool, left = sum([portions[i] for i in candidates]), spare
        for i in candidates:
            extra = min(limit - counts[i], max(1, left * portions[i] // pool), spare)
            counts[i] = counts[i] + extra
            spare = spare - extra
    return np.array(counts)


def noise(key, extent, scale, bound, shards=(), held_as=jnp.bfloat16):
    entries = jax.random.normal(key, extent, jnp.float32) * scale
    if len(shards) > 0:
        entries = block_levels(key, extent, shards, -0.22, 0.18) * entries
    return jnp.clip(entries, min=-bound, max=bound).astype(held_as)


def gaussian_with(key, extent, deviation, most, split, heavy, held_as=jnp.bfloat16):
    values = deviation * jax.random.normal(key, extent, jnp.float32)
    if split:
        values = values * block_levels(key, extent, split, -0.22, 0.18)
    return jnp.clip(strengthened(values, jax.random.fold_in(key, 3), *heavy), -most, most).astype(held_as)


def setup_inputs(seed: int = 0) -> dict:
    arg_keys = jax.random.split(jax.random.key(seed), 18)
    query = noise(arg_keys[0], (REQS, STEPS, HEADS * DK), 1.0, 6.0, ((0, 4), (2, 8)))
    key_in = noise(arg_keys[1], (REQS, STEPS, HEADS * DK), 1.0, 6.0, ((0, 4), (2, 8)))
    value = noise(arg_keys[2], (REQS, STEPS, HEADS * DV), 1.0, 6.0, ((0, 4), (2, 8)))
    gate_z = noise(arg_keys[3], (REQS, STEPS, HEADS * DV), 1.0, 6.0, ((0, 4), (2, 8)))
    alpha_in = noise(arg_keys[4], (REQS, STEPS, HEADS), 1.0, 6.0, ((0, 4), (2, 8)), jnp.float32)
    beta_in = noise(arg_keys[5], (REQS, STEPS, HEADS), 1.5, 9.0, ((0, 4), (2, 8)), jnp.float32)
    a_log = jnp.clip(-2.0 + 2.5 * jax.random.uniform(arg_keys[6], (HEADS,), jnp.float32) ** block_levels(arg_keys[6], (HEADS,), ((0, 8),), -0.2, 0.2), -2.0, 0.5)
    dt_bias = jnp.clip(jax.random.uniform(arg_keys[7], (HEADS,), jnp.float32, -1.0, 1.0) * block_levels(arg_keys[7], (HEADS,), ((0, 8),), -0.4, 0.0), -1.0, 1.0)
    norm_gain = jnp.clip(jax.random.uniform(arg_keys[8], (DV,), jnp.float32, 0.5, 1.5), 0.5, 1.5)
    state = noise(arg_keys[9], (REQS, HEADS, DK, DV), 1.0, 6.0, ((0, 4), (1, 8)))
    out_weight = gaussian_with(arg_keys[10], (HEADS * DV, D), (HEADS * DV) ** -0.5, 0.125, ((0, 8),), (0, 1, 8, 2.0))
    hidden = noise(arg_keys[11], (REQS, STEPS, D), 1.0, 6.0, ((0, 4),))
    post_gain = jnp.clip(jax.random.uniform(arg_keys[12], (D,), jnp.float32, 0.5, 1.5), 0.5, 1.5)
    expert_in = noise(arg_keys[13], (2 * EXPERTS, D, 2 * HALF), D ** -0.5, 0.125, ((0, 32),))
    expert_out = noise(arg_keys[14], (2 * EXPERTS, HALF, D), (2 * HALF) ** -0.5, 0.25, ((0, 32),))
    expert_ids_keys = jax.random.split(jax.random.fold_in(arg_keys[15], 1), REQS * STEPS // (R_DEV * STEPS))
    expert_ids_turns = jax.random.permutation(jax.random.fold_in(arg_keys[15], 3), REQS * STEPS // (R_DEV * STEPS))
    expert_ids = jax.vmap(lambda own, number: routed_block(jax.random.fold_in(arg_keys[15], 2), own, number, R_DEV * STEPS, EXPERTS, TOPK, MOST, 2))(expert_ids_keys, expert_ids_turns).reshape((REQS, STEPS, TOPK))
    route_weights = jnp.clip(0.049804688 + 0.24902344 * jax.random.uniform(arg_keys[16], (REQS, STEPS, TOPK), jnp.float32) ** block_levels(arg_keys[16], (REQS, STEPS, TOPK), ((0, 4),), -0.2, 0.2), 0.049804688, 0.29882812).astype(jnp.bfloat16)
    return dict(query=query, key_in=key_in, value=value, gate_z=gate_z, alpha_in=alpha_in, beta_in=beta_in, a_log=a_log, dt_bias=dt_bias, norm_gain=norm_gain, state=state, out_weight=out_weight, hidden=hidden, post_gain=post_gain, expert_in=expert_in, expert_out=expert_out, expert_ids=expert_ids, route_weights=route_weights)


def unit_rows(values):
    return values * lax.rsqrt(lax.optimization_barrier(jnp.sum(values * values, axis=-1, keepdims=True)) + 1e-06)

def recur(query, key_in, value, gate_z, alpha_in, beta_in, a_log, dt_bias, norm_gain, state):
    requests, positions, head_count = alpha_in.shape
    key_size = state.shape[2]
    value_size = state.shape[3]
    queries = query.astype(jnp.float32).reshape(requests, positions, head_count, key_size)
    key_rows = key_in.astype(jnp.float32).reshape(requests, positions, head_count, key_size)
    value_rows = value.astype(jnp.float32).reshape(requests, positions, head_count, value_size)
    memory = state.astype(jnp.float32)
    decay_scale = -jnp.exp(a_log)
    outputs = []
    for position in range(positions):
        query_unit = unit_rows(queries[:, position]) * key_size ** (-0.5)
        key_unit = unit_rows(key_rows[:, position])
        decay_rate = jnp.exp(decay_scale * jax.nn.softplus(alpha_in[:, position] + dt_bias))
        write_rate = jax.nn.sigmoid(beta_in[:, position])
        memory = memory * decay_rate[:, :, None, None]
        recalled = jnp.einsum('rhk,rhkv->rhv', key_unit, memory, precision=lax.Precision.HIGHEST)
        correction = (value_rows[:, position] - recalled) * write_rate[:, :, None]
        memory = memory + key_unit[:, :, :, None] * correction[:, :, None, :]
        outputs.append(jnp.einsum('rhk,rhkv->rhv', query_unit, memory, precision=lax.Precision.HIGHEST))
    head_out = jnp.stack(outputs, axis=1)
    scaled = head_out * lax.rsqrt(lax.optimization_barrier(jnp.mean(head_out * head_out, axis=-1, keepdims=True)) + 1e-06) * norm_gain
    gate_rows = gate_z.astype(jnp.float32).reshape(requests, positions, head_count, value_size)
    gated_out = (scaled * jax.nn.silu(gate_rows)).astype(jnp.bfloat16)
    return gated_out.reshape(requests * positions, head_count * value_size)

def reference(query, key_in, value, gate_z, alpha_in, beta_in, a_log, dt_bias, norm_gain, state, out_weight, hidden, post_gain, expert_in, expert_out, expert_ids, route_weights):
    gated_out = recur(query, key_in, value, gate_z, alpha_in, beta_in, a_log, dt_bias, norm_gain, state)
    projected = jnp.dot(gated_out, out_weight, preferred_element_type=jnp.float32)
    after_mixer = hidden.reshape(REQS * STEPS, D).astype(jnp.float32) + projected
    normed = (after_mixer * lax.rsqrt(lax.optimization_barrier(jnp.mean(after_mixer * after_mixer, axis=1, keepdims=True)) + 1e-06) * post_gain).astype(jnp.bfloat16)
    group_rows = R_DEV * STEPS
    grouped = normed.reshape(N_REQ, group_rows, D).astype(jnp.float32)
    ids_grouped = expert_ids.reshape(N_REQ, group_rows, TOPK)
    weights_grouped = route_weights.reshape(N_REQ, group_rows, TOPK).astype(jnp.float32)
    slot_ids = lax.broadcasted_iota(jnp.int32, (1, 1, MOST), 2)

    def one_expert(carry, expert):
        hits = ids_grouped == expert
        member = jnp.any(hits, axis=-1).astype(jnp.int32)
        picked = lax.optimization_barrier(jnp.sum(jnp.where(hits, weights_grouped, 0.0), axis=-1))
        before = jnp.cumsum(member, axis=1) - member
        placed = ((member[:, :, None] == 1) & (before[:, :, None] == slot_ids)).astype(jnp.float32)
        gathered = jnp.einsum('gnc,gnf->gcf', placed, grouped).astype(jnp.bfloat16).reshape(N_REQ * MOST, D)
        weighted = placed * picked[:, :, None]
        for half_index in range(2):
            row_index = (2 * expert + half_index).astype(jnp.int32)
            weight_in = lax.dynamic_index_in_dim(expert_in, row_index, 0, keepdims=False)
            weight_out = lax.dynamic_index_in_dim(expert_out, row_index, 0, keepdims=False)
            proj_rows = jnp.dot(gathered, weight_in, preferred_element_type=jnp.float32)
            inner = (jax.nn.silu(proj_rows[:, :HALF]) * proj_rows[:, HALF:]).astype(jnp.bfloat16)
            half_out = jnp.dot(inner, weight_out, preferred_element_type=jnp.float32).astype(jnp.bfloat16)
            half_out = half_out.reshape(N_REQ, MOST, D).astype(jnp.float32)
            carry = carry + jnp.einsum('gnc,gcf->gnf', weighted, half_out)
        return (carry, None)
    start = jnp.zeros((N_REQ, group_rows, D), jnp.float32)
    expert_sum, _ = lax.scan(one_expert, start, jnp.arange(EXPERTS, dtype=jnp.int32))
    mixed = (after_mixer + expert_sum.reshape(REQS * STEPS, D)).astype(jnp.bfloat16)
    return mixed.reshape(REQS, STEPS, D)
```

```python
import jax
import jax.numpy as jnp
from jax import lax
from jax.experimental import pallas as pl
from jax.experimental.pallas import tpu as pltpu
from jax.sharding import PartitionSpec as P

MOST = 4
TOPK = 10


def unit_rows(values):
    return values * lax.rsqrt(jnp.sum(values * values, axis=-1, keepdims=True) + 1e-06)


def recur(query, key_in, value, gate_z, alpha_in, beta_in, a_log, dt_bias, norm_gain, state):
    requests, positions, head_count = alpha_in.shape
    key_size = state.shape[2]
    value_size = state.shape[3]
    queries = query.astype(jnp.float32).reshape(requests, positions, head_count, key_size)
    key_rows = key_in.astype(jnp.float32).reshape(requests, positions, head_count, key_size)
    value_rows = value.astype(jnp.float32).reshape(requests, positions, head_count, value_size)
    memory = state.astype(jnp.float32)
    decay_scale = -jnp.exp(a_log)
    outputs = []
    for position in range(positions):
        query_unit = unit_rows(queries[:, position]) * key_size ** (-0.5)
        key_unit = unit_rows(key_rows[:, position])
        decay_rate = jnp.exp(decay_scale * jax.nn.softplus(alpha_in[:, position] + dt_bias))
        write_rate = jax.nn.sigmoid(beta_in[:, position])
        memory = memory * decay_rate[:, :, None, None]
        recalled = jnp.einsum("rhk,rhkv->rhv", key_unit, memory, precision=lax.Precision.HIGHEST)
        correction = (value_rows[:, position] - recalled) * write_rate[:, :, None]
        memory = memory + key_unit[:, :, :, None] * correction[:, :, None, :]
        outputs.append(
            jnp.einsum("rhk,rhkv->rhv", query_unit, memory, precision=lax.Precision.HIGHEST)
        )
    head_out = jnp.stack(outputs, axis=1)
    scaled = (
        head_out
        * lax.rsqrt(jnp.mean(head_out * head_out, axis=-1, keepdims=True) + 1e-06)
        * norm_gain
    )
    gate_rows = gate_z.astype(jnp.float32).reshape(requests, positions, head_count, value_size)
    gated_out = (scaled * jax.nn.silu(gate_rows)).astype(jnp.bfloat16)
    return gated_out.reshape(requests * positions, head_count * value_size)


def route_tables(ids_flat, weights_flat, targets):
    hits = ids_flat[:, :, None] == targets[None, None, :]
    member = jnp.any(hits, axis=1).astype(jnp.int32)
    picked = jnp.sum(jnp.where(hits, weights_flat.astype(jnp.float32)[:, :, None], 0.0), axis=1)
    before = jnp.cumsum(member, axis=0) - member
    slot_ids = lax.broadcasted_iota(jnp.int32, (1, 1, MOST), 2)
    placed = (member[:, :, None] == 1) & (before[:, :, None] == slot_ids)
    return (placed, picked)


def run_experts(received, expert_in, expert_out):
    projected = jnp.einsum(
        "rjcd,jdf->rjcf", received, expert_in, preferred_element_type=jnp.float32
    )
    half_units = expert_out.shape[1]
    inner = (jax.nn.silu(projected[..., :half_units]) * projected[..., half_units:]).astype(
        jnp.bfloat16
    )
    return jnp.einsum(
        "rjch,jhd->rjcd", inner, expert_out, preferred_element_type=jnp.float32
    ).astype(jnp.bfloat16)


def on_device(
    query,
    key_in,
    value,
    gate_z,
    alpha_in,
    beta_in,
    a_log,
    dt_bias,
    norm_gain,
    state,
    out_weight,
    hidden,
    post_gain,
    expert_in,
    expert_out,
    expert_ids,
    route_weights,
):
    requests, positions, width = hidden.shape
    row_count = requests * positions
    gated_out = recur(
        query, key_in, value, gate_z, alpha_in, beta_in, a_log, dt_bias, norm_gain, state
    )
    partial_value = jnp.dot(gated_out, out_weight, preferred_element_type=jnp.float32)
    ids_flat = expert_ids.reshape(row_count, -1)
    weights_flat = route_weights.reshape(row_count, -1)
    req_count = lax.axis_size("req")
    ep_count = lax.axis_size("ep")
    ep_index = lax.axis_index("ep")
    per_device = expert_in.shape[0]
    slice_width = width // ep_count
    residual = hidden.reshape(row_count, width).astype(jnp.float32)
    projected_sum = lax.psum(partial_value.astype(jnp.bfloat16), "ep").astype(jnp.float32)
    after_mixer = residual + projected_sum
    normed = (
        after_mixer
        * lax.rsqrt(jnp.mean(after_mixer * after_mixer, axis=1, keepdims=True) + 1e-06)
        * post_gain
    ).astype(jnp.bfloat16)
    mixer_share = lax.dynamic_slice_in_dim(after_mixer, ep_index * slice_width, slice_width, 1)
    groups = lax.broadcasted_iota(jnp.int32, (req_count, per_device), 0)
    halves = lax.broadcasted_iota(jnp.int32, (req_count, per_device), 1)
    targets = (((groups * ep_count + ep_index) * per_device + halves) // 2).reshape(-1)
    placed, picked = route_tables(ids_flat, weights_flat, targets)
    outgoing = jnp.einsum(
        "ndc,nf->dcf", placed.astype(jnp.bfloat16), normed, preferred_element_type=jnp.float32
    )
    outgoing = outgoing.astype(jnp.bfloat16).reshape(req_count, per_device, MOST, width)
    served = run_experts(
        lax.all_to_all(outgoing, "req", split_axis=0, concat_axis=0, tiled=True),
        expert_in,
        expert_out,
    )
    returned = lax.all_to_all(served, "req", split_axis=0, concat_axis=0, tiled=True)
    combine_weights = (placed * picked[:, :, None]).astype(jnp.bfloat16).reshape(row_count, -1)
    expert_rows = jnp.dot(
        combine_weights, returned.reshape(-1, width), preferred_element_type=jnp.float32
    )
    expert_share = lax.psum_scatter(
        expert_rows.astype(jnp.bfloat16), "ep", scatter_dimension=1, tiled=True
    ).astype(jnp.float32)
    mixed = (mixer_share + expert_share).astype(jnp.bfloat16)
    return mixed.reshape(requests, positions, slice_width)


MESH = pl.DeviceIdType.MESH
VMEM_LIMIT = 58 * 1024 * 1024


def mixer_kernel(q_ref, k_ref, v_ref, z_ref, rates_ref, gain_ref, state_ref, weight_ref, out_ref, rows, reads, total):
    head = pl.program_id(0)
    requests = q_ref.shape[0]
    rows[:, 0:2, :] = k_ref[...].astype(jnp.float32)
    rows[:, 2:4, :] = q_ref[...].astype(jnp.float32)
    rows[:, 4:6, :] = v_ref[...].astype(jnp.float32)
    rows[:, 6:8, :] = z_ref[...].astype(jnp.float32)
    reads[...] = lax.dot_general(
        rows[...].astype(jnp.bfloat16),
        state_ref[...].reshape(requests, state_ref.shape[2], state_ref.shape[3]),
        (((2,), (1,)), ((0,), (0,))),
        preferred_element_type=jnp.float32,
    )
    key0, key1, query0, query1 = (rows[:, i, :] for i in range(4))
    value0, value1, gate0, gate1 = (rows[:, i, :] for i in range(4, 8))

    def dot(a, b):
        return jnp.sum(a * b, axis=-1, keepdims=True)

    scale = q_ref.shape[2] ** (-0.5)
    kn0 = lax.rsqrt(dot(key0, key0) + 1e-06)
    kn1 = lax.rsqrt(dot(key1, key1) + 1e-06)
    qn0 = lax.rsqrt(dot(query0, query0) + 1e-06) * scale
    qn1 = lax.rsqrt(dot(query1, query1) + 1e-06) * scale
    rates = rates_ref[...].reshape(requests, 4)
    decay0, decay1, write0, write1 = (rates[:, i : i + 1] for i in range(4))
    change0 = (value0 - (decay0 * kn0) * reads[:, 0, :]) * write0
    head0 = (decay0 * qn0) * reads[:, 2, :] + (dot(query0, key0) * qn0 * kn0) * change0
    both = decay0 * decay1
    recalled1 = (both * kn1) * reads[:, 1, :] + (decay1 * dot(key1, key0) * kn1 * kn0) * change0
    change1 = (value1 - recalled1) * write1
    head1 = (
        (both * qn1) * reads[:, 3, :]
        + (decay1 * dot(query1, key0) * qn1 * kn0) * change0
        + (dot(query1, key1) * qn1 * kn1) * change1
    )
    gain = gain_ref[...]

    def finish(out, gate):
        mean = jnp.mean(out * out, axis=-1, keepdims=True)
        return out * lax.rsqrt(mean + 1e-06) * gain * (gate * jax.nn.sigmoid(gate))

    gated = jnp.concatenate([finish(head0, gate0), finish(head1, gate1)], axis=0).astype(jnp.bfloat16)
    part = jnp.dot(gated, weight_ref[...], preferred_element_type=jnp.float32)

    @pl.when(head == 0)
    def _():
        total[...] = part

    @pl.when(head > 0)
    def _():
        total[...] += part

    @pl.when(head == pl.num_programs(0) - 1)
    def _():
        slices, _, width = out_ref.shape
        for s in range(slices):
            out_ref[s] = total[:, s * width : (s + 1) * width].astype(jnp.bfloat16)


def mixer(query, key_in, value, gate_z, rates, norm_gain, state, out_weight, slices):
    requests, positions, _ = query.shape
    heads, key_size, value_size = state.shape[1:]
    width = out_weight.shape[1]
    rows = requests * positions
    row_spec = pl.BlockSpec((requests, positions, key_size), lambda h: (0, 0, h))
    return pl.pallas_call(
        mixer_kernel,
        grid=(heads,),
        out_shape=jax.ShapeDtypeStruct((slices, rows, width // slices), jnp.bfloat16),
        in_specs=[
            row_spec,
            row_spec,
            row_spec,
            row_spec,
            pl.BlockSpec((1, requests, 4), lambda h: (h, 0, 0)),
            pl.BlockSpec((1, value_size), lambda h: (0, 0)),
            pl.BlockSpec((requests, 1, key_size, value_size), lambda h: (0, h, 0, 0)),
            pl.BlockSpec((value_size, width), lambda h: (h, 0)),
        ],
        out_specs=pl.BlockSpec((slices, rows, width // slices), lambda h: (0, 0, 0)),
        scratch_shapes=[
            pltpu.VMEM((requests, 8, key_size), jnp.float32),
            pltpu.VMEM((requests, 8, value_size), jnp.float32),
            pltpu.VMEM((rows, width), jnp.float32),
        ],
        compiler_params=pltpu.CompilerParams(vmem_limit_bytes=VMEM_LIMIT),
        name="mixer",
    )(query, key_in, value, gate_z, rates, norm_gain.reshape(1, -1), state, out_weight)


def expert_kernel(
    part_ref, hidden_ref, gain_ref, table_ref, win_hbm, wout_hbm, out_ref,
    win, wout, rs_buf, after, xall, tables, slots, served, combine,
    send_a, recv_a, own, send_b, recv_b, total, send_c, recv_c,
    w_sem, rs_send, rs_recv, tab_send, tab_recv, z_send, z_recv, pl_send, pl_recv,
    fw_send, fw_recv, a_send, a_recv, b_send, b_recv, c_send, c_recv,
):
    z = lax.axis_index("req")
    me = lax.axis_index("ep")
    core = lax.rem(me, 2)
    chip = me // 2
    chip_x = lax.rem(chip, 2)
    chip_y = chip // 2
    experts = win.shape[0] // 2
    rows, width = after.shape

    def chip_at(m):
        return lax.rem(chip_y + m // 2, 2) * 2 + lax.rem(chip_x + m % 2, 2)

    def mate(m):
        return chip_at(m // 2) * 2 + lax.rem(core + m % 2, 2)

    def level(k):
        return lax.rem(z + k, 4)

    def remote(src, dst, send, recv, device):
        return pltpu.make_async_remote_copy(
            src_ref=src, dst_ref=dst, send_sem=send, recv_sem=recv, device_id=device, device_id_type=MESH
        )

    def weight_copies(e):
        pair = pl.ds(2 * e, 2)
        return (
            pltpu.make_async_copy(win_hbm.at[pair], win.at[pair], w_sem.at[0, e]),
            pltpu.make_async_copy(wout_hbm.at[pair], wout.at[pair], w_sem.at[1, e]),
        )

    barrier = pltpu.get_barrier_semaphore()
    for m in range(1, 8):
        pl.semaphore_signal(barrier, inc=1, device_id=(z, mate(m)), device_id_type=MESH)
    for k in range(1, 4):
        pl.semaphore_signal(barrier, inc=1, device_id=(level(k), me), device_id_type=MESH)
    for e in range(experts):
        for copy in weight_copies(e):
            copy.start()
    tables[0] = table_ref[...]
    pl.semaphore_wait(barrier, 10)
    sent = []

    for m in (6, 7, 2, 3, 4, 5, 1):
        copy = remote(part_ref.at[mate(m)], rs_buf.at[m - 1], rs_send.at[m - 1], rs_recv.at[m - 1], (z, mate(m)))
        copy.start()
        sent.append(copy)
    for k in range(1, 4):
        copy = remote(table_ref, tables.at[k], tab_send.at[k - 1], tab_recv.at[k - 1], (level(k), me))
        copy.start()
        sent.append(copy)
    total_rows = part_ref[me].astype(jnp.float32) + hidden_ref[...].astype(jnp.float32)
    for m in (1, 2, 3, 4, 5, 6, 7):
        remote(rs_buf.at[m - 1], rs_buf.at[m - 1], rs_send.at[m - 1], rs_recv.at[m - 1], (z, mate(m))).wait_recv()
        total_rows = total_rows + rs_buf[m - 1].astype(jnp.float32)
    after[...] = total_rows
    xall[0, me] = total_rows.astype(jnp.bfloat16)

    for k in (3, 2, 1):
        copy = remote(xall.at[0, me], xall.at[k, me], z_send.at[k - 1], z_recv.at[k - 1], (level(k), me))
        copy.start()
        sent.append(copy)
    near = (6, 2, 4, 1)
    for k in range(4):
        if k:
            remote(xall.at[k, me], xall.at[k, me], z_send.at[k - 1], z_recv.at[k - 1], (level(k), me)).wait_recv()
        for i, m in enumerate(near):
            copy = remote(xall.at[k, me], xall.at[k, me], pl_send.at[k, i], pl_recv.at[k, i], (z, mate(m)))
            copy.start()
            sent.append(copy)

    for k in range(1, 4):
        remote(tables.at[k], tables.at[k], tab_send.at[k - 1], tab_recv.at[k - 1], (level(k), me)).wait_recv()
    all_rows = 4 * rows
    listed = jnp.concatenate([tables[0] + tables[1], tables[2] + tables[3]], axis=1)
    odd = lax.rem(z, 2)
    column = lax.broadcasted_iota(jnp.int32, (1, all_rows), 1) // rows
    group_of = 2 * (column // 2) + lax.rem(column + odd, 2)
    ep_count = xall.shape[1]
    first = ((z * ep_count + me) * experts).astype(jnp.float32)
    names = first + lax.broadcasted_iota(jnp.int32, (experts, all_rows), 0).astype(jnp.float32)
    member = jnp.zeros((experts, all_rows), jnp.float32)
    picked = jnp.zeros((experts, all_rows), jnp.float32)
    for t in range(TOPK):
        hit = listed[t : t + 1, :] == names
        member = member + jnp.where(hit, 1.0, 0.0)
        picked = picked + jnp.where(hit, listed[16 + t : 17 + t, :], 0.0)
    earlier = lax.broadcasted_iota(jnp.int32, (all_rows, all_rows), 0)
    later = lax.broadcasted_iota(jnp.int32, (all_rows, all_rows), 1)
    precedes = jnp.where((earlier < later) & (earlier // rows == later // rows), 1.0, 0.0)
    before = jnp.dot(member.astype(jnp.bfloat16), precedes.astype(jnp.bfloat16), preferred_element_type=jnp.float32)
    code = jnp.where(member > 0.5, before + (MOST * group_of).astype(jnp.float32), -1.0)
    spots = 4 * MOST
    places = lax.broadcasted_iota(jnp.int32, (experts, spots, all_rows), 1).astype(jnp.float32)
    placed = jnp.where(code[:, None, :] == places, 1.0, 0.0)
    weighted = (placed * picked[:, None, :]).reshape(experts * spots, all_rows)
    placed = placed.reshape(experts * spots, all_rows).astype(jnp.bfloat16)
    combine[...] = weighted.T.astype(jnp.bfloat16)

    for k in range(4):
        for i in range(3):
            other = mate(near[i])
            remote(xall.at[k, other], xall.at[k, other], pl_send.at[k, i], pl_recv.at[k, i], (z, other)).wait_recv()
            copy = remote(xall.at[k, other], xall.at[k, other], fw_send.at[k, i], fw_recv.at[k, i], (z, mate(1)))
            copy.start()
            sent.append(copy)
    for k in range(4):
        remote(xall.at[k, mate(1)], xall.at[k, mate(1)], pl_send.at[k, 3], pl_recv.at[k, 3], (z, mate(1))).wait_recv()
        for i in range(3):
            other = mate(near[i] + 1)
            remote(xall.at[k, other], xall.at[k, other], fw_send.at[k, i], fw_recv.at[k, i], (z, mate(1))).wait_recv()

    squares = jnp.zeros((experts * spots, 1), jnp.float32)
    raw = []
    for s in range(ep_count):
        first_pair = jnp.concatenate([xall[odd, s], xall[1 - odd, s]], axis=0)
        second_pair = jnp.concatenate([xall[2 + odd, s], xall[3 - odd, s]], axis=0)
        block = jnp.concatenate([first_pair, second_pair], axis=0)
        picked_rows = jnp.dot(placed, block, preferred_element_type=jnp.float32)
        squares = squares + jnp.sum(picked_rows * picked_rows, axis=1, keepdims=True)
        slots[:, :, s * width : (s + 1) * width] = picked_rows.astype(jnp.bfloat16).reshape(experts, spots, width)
    unit = lax.rsqrt(squares * (1.0 / (ep_count * width)) + 1e-06).reshape(experts, spots, 1)
    for s in range(ep_count):
        part = slots[:, :, s * width : (s + 1) * width].astype(jnp.float32)
        gain = gain_ref[:, s * width : (s + 1) * width].reshape(1, 1, width)
        slots[:, :, s * width : (s + 1) * width] = (part * unit * gain).astype(jnp.bfloat16)

    half = wout.shape[1]

    def one_expert(e, carry):
        for copy in weight_copies(e):
            copy.wait()
        x = slots[e]
        sums = None
        for j in range(2):
            proj = jnp.dot(x, win[2 * e + j], preferred_element_type=jnp.float32)
            gate = proj[:, :half]
            inner = (gate * jax.nn.sigmoid(gate) * proj[:, half:]).astype(jnp.bfloat16)
            term = jnp.dot(inner, wout[2 * e + j], preferred_element_type=jnp.float32)
            sums = term if sums is None else sums + term
        served[e] = sums.astype(jnp.bfloat16)
        return carry

    lax.fori_loop(0, experts, one_expert, 0)

    def weigh(column_slice):
        block = served[:, :, pl.ds(pl.multiple_of(column_slice * width, width), width)]
        return jnp.dot(
            combine[...], block.reshape(experts * spots, width), preferred_element_type=jnp.float32
        )

    order = (3, 1, 2, 0)
    for c in order:
        send_a[c] = weigh(chip_at(c) * 2 + 1 - core).astype(jnp.bfloat16)
        copy = remote(send_a.at[c], recv_a.at[c], a_send.at[c], a_recv.at[c], (z, mate(1)))
        copy.start()
        sent.append(copy)
    for c in order:
        own[c] = weigh(chip_at(c) * 2 + core)
    for c in order:
        remote(recv_a.at[c], recv_a.at[c], a_send.at[c], a_recv.at[c], (z, mate(1))).wait_recv()
        both = own[c] + recv_a[c].astype(jnp.float32)
        if c == 0:
            total[...] = both
        else:
            send_b[c - 1] = both.astype(jnp.bfloat16)
            for q in range(4):
                span = pl.ds(q * rows, rows)
                copy = remote(
                    send_b.at[c - 1, span], recv_b.at[c - 1, span],
                    b_send.at[c - 1, q], b_recv.at[c - 1, q], (z, mate(2 * c)),
                )
                copy.start()
                sent.append(copy)
    result = after[...]
    for q in range(4):
        span = pl.ds(q * rows, rows)
        for c in (1, 2, 3):
            remote(
                recv_b.at[c - 1, span], recv_b.at[c - 1, span],
                b_send.at[c - 1, q], b_recv.at[c - 1, q], (z, mate(2 * c)),
            ).wait_recv()
            total[span, :] += recv_b[c - 1, span, :].astype(jnp.float32)
    for k in (3, 2, 1):
        block = 2 * (k // 2) + lax.rem(k + odd, 2)
        start = pl.multiple_of(block * rows, rows)
        send_c[k - 1] = total[pl.ds(start, rows), :].astype(jnp.bfloat16)
        copy = remote(
            send_c.at[k - 1], recv_c.at[k - 1], c_send.at[k - 1], c_recv.at[k - 1], (level(4 - k), me)
        )
        copy.start()
        sent.append(copy)
    result = result + total[pl.ds(pl.multiple_of(odd * rows, rows), rows), :]
    for k in (1, 2, 3):
        remote(
            recv_c.at[k - 1], recv_c.at[k - 1], c_send.at[k - 1], c_recv.at[k - 1], (level(k), me)
        ).wait_recv()
        result = result + recv_c[k - 1].astype(jnp.float32)
    out_ref[...] = result.astype(jnp.bfloat16)
    for copy in sent:
        copy.wait_send()


def serve(part, hidden_rows, post_gain, table, expert_in, expert_out):
    slices, rows, width = part.shape
    halves, features, columns = expert_in.shape
    half = expert_out.shape[1]
    experts = halves // 2
    spots = 4 * MOST
    bf16, f32 = jnp.bfloat16, jnp.float32
    vmem, dma = pltpu.VMEM, pltpu.SemaphoreType.DMA
    in_vmem = pl.BlockSpec(memory_space=pltpu.VMEM)
    in_hbm = pl.BlockSpec(memory_space=pl.ANY)
    return pl.pallas_call(
        expert_kernel,
        out_shape=jax.ShapeDtypeStruct((rows, width), bf16),
        in_specs=[in_vmem] * 4 + [in_hbm] * 2,
        out_specs=in_vmem,
        scratch_shapes=[
            vmem((halves, features, columns), bf16),
            vmem((halves, half, features), bf16),
            vmem((slices - 1, rows, width), bf16),
            vmem((rows, width), f32),
            vmem((4, slices, rows, width), bf16),
            vmem((4,) + table.shape, f32),
            vmem((experts, spots, features), bf16),
            vmem((experts, spots, features), bf16),
            vmem((4 * rows, experts * spots), bf16),
            vmem((4, 4 * rows, width), bf16),
            vmem((4, 4 * rows, width), bf16),
            vmem((4, 4 * rows, width), f32),
            vmem((3, 4 * rows, width), bf16),
            vmem((3, 4 * rows, width), bf16),
            vmem((4 * rows, width), f32),
            vmem((3, rows, width), bf16),
            vmem((3, rows, width), bf16),
            dma((2, experts)),
            dma((7,)), dma((7,)),
            dma((3,)), dma((3,)),
            dma((3,)), dma((3,)),
            dma((4, 4)), dma((4, 4)),
            dma((4, 3)), dma((4, 3)),
            dma((4,)), dma((4,)),
            dma((3, 4)), dma((3, 4)),
            dma((3,)), dma((3,)),
        ],
        compiler_params=pltpu.CompilerParams(
            collective_id=0, has_side_effects=True, vmem_limit_bytes=VMEM_LIMIT
        ),
        name="experts",
    )(part, hidden_rows, post_gain.reshape(1, -1), table, expert_in, expert_out)


def in_kernels(
    query, key_in, value, gate_z, alpha_in, beta_in, a_log, dt_bias, norm_gain, state,
    out_weight, hidden, post_gain, expert_in, expert_out, expert_ids, route_weights,
):
    requests, positions, width = hidden.shape
    rows = requests * positions
    ep_count = lax.axis_size("ep")
    slice_width = width // ep_count
    decay = jnp.exp(-jnp.exp(a_log) * jax.nn.softplus(alpha_in + dt_bias))
    rates = jnp.concatenate([decay, jax.nn.sigmoid(beta_in)], axis=1).transpose(2, 0, 1)
    part = mixer(query, key_in, value, gate_z, rates, norm_gain, state, out_weight, ep_count)
    hidden_rows = lax.dynamic_slice_in_dim(hidden, lax.axis_index("ep") * slice_width, slice_width, 2)
    hidden_rows = hidden_rows.transpose(1, 0, 2).reshape(rows, slice_width)

    def lanes(values):
        listed = values.astype(jnp.float32).transpose(2, 1, 0).reshape(TOPK, rows)
        return jnp.pad(listed, ((0, 16 - TOPK), (0, 0)))

    listed = jnp.concatenate([lanes(expert_ids), lanes(route_weights)], axis=0)
    odd = lax.axis_index("req") % 2 == 1
    table = jnp.concatenate([jnp.where(odd, 0.0, listed), jnp.where(odd, listed, 0.0)], axis=1)
    mixed = serve(part, hidden_rows, post_gain, table, expert_in, expert_out)
    return mixed.reshape(positions, requests, slice_width).transpose(1, 0, 2)


def solution(mesh):
    body = in_kernels if mesh.shape["req"] == 4 and mesh.shape["ep"] == 8 else on_device
    return jax.shard_map(
        body,
        mesh=mesh,
        in_specs=(
            P("req", None, "ep"),
            P("req", None, "ep"),
            P("req", None, "ep"),
            P("req", None, "ep"),
            P("req", None, "ep"),
            P("req", None, "ep"),
            P("ep"),
            P("ep"),
            P(),
            P("req", "ep", None, None),
            P("ep", None),
            P("req", None, None),
            P(),
            P(("req", "ep"), None, None),
            P(("req", "ep"), None, None),
            P("req", None, None),
            P("req", None, None),
        ),
        out_specs=P("req", None, "ep"),
        check_vma=False,
    )
```

```python
import jax
import jax.numpy as jnp
from jax import lax
from jax.experimental import pallas as pl
from jax.experimental.pallas import tpu as pltpu
from jax.sharding import PartitionSpec as P

MOST = 4


def unit_rows(values):
    return values * lax.rsqrt(jnp.sum(values * values, axis=-1, keepdims=True) + 1e-06)


def recur(query, key_in, value, gate_z, alpha_in, beta_in, a_log, dt_bias, norm_gain, state):
    requests, positions, head_count = alpha_in.shape
    key_size = state.shape[2]
    value_size = state.shape[3]
    queries = query.astype(jnp.float32).reshape(requests, positions, head_count, key_size)
    key_rows = key_in.astype(jnp.float32).reshape(requests, positions, head_count, key_size)
    value_rows = value.astype(jnp.float32).reshape(requests, positions, head_count, value_size)
    memory = state.astype(jnp.float32)
    decay_scale = -jnp.exp(a_log)
    outputs = []
    for position in range(positions):
        query_unit = unit_rows(queries[:, position]) * key_size ** (-0.5)
        key_unit = unit_rows(key_rows[:, position])
        decay_rate = jnp.exp(decay_scale * jax.nn.softplus(alpha_in[:, position] + dt_bias))
        write_rate = jax.nn.sigmoid(beta_in[:, position])
        memory = memory * decay_rate[:, :, None, None]
        recalled = jnp.einsum("rhk,rhkv->rhv", key_unit, memory, precision=lax.Precision.HIGHEST)
        correction = (value_rows[:, position] - recalled) * write_rate[:, :, None]
        memory = memory + key_unit[:, :, :, None] * correction[:, :, None, :]
        outputs.append(
            jnp.einsum("rhk,rhkv->rhv", query_unit, memory, precision=lax.Precision.HIGHEST)
        )
    head_out = jnp.stack(outputs, axis=1)
    scaled = (
        head_out
        * lax.rsqrt(jnp.mean(head_out * head_out, axis=-1, keepdims=True) + 1e-06)
        * norm_gain
    )
    gate_rows = gate_z.astype(jnp.float32).reshape(requests, positions, head_count, value_size)
    gated_out = (scaled * jax.nn.silu(gate_rows)).astype(jnp.bfloat16)
    return gated_out.reshape(requests * positions, head_count * value_size)


def route_tables(ids_flat, weights_flat, targets):
    hits = ids_flat[:, :, None] == targets[None, None, :]
    member = jnp.any(hits, axis=1).astype(jnp.int32)
    picked = jnp.sum(jnp.where(hits, weights_flat.astype(jnp.float32)[:, :, None], 0.0), axis=1)
    before = jnp.cumsum(member, axis=0) - member
    slot_ids = lax.broadcasted_iota(jnp.int32, (1, 1, MOST), 2)
    placed = (member[:, :, None] == 1) & (before[:, :, None] == slot_ids)
    return (placed, picked)


def run_experts(received, expert_in, expert_out):
    projected = jnp.einsum(
        "rjcd,jdf->rjcf", received, expert_in, preferred_element_type=jnp.float32
    )
    half_units = expert_out.shape[1]
    inner = (jax.nn.silu(projected[..., :half_units]) * projected[..., half_units:]).astype(
        jnp.bfloat16
    )
    return jnp.einsum(
        "rjch,jhd->rjcd", inner, expert_out, preferred_element_type=jnp.float32
    ).astype(jnp.bfloat16)


def on_device(
    query,
    key_in,
    value,
    gate_z,
    alpha_in,
    beta_in,
    a_log,
    dt_bias,
    norm_gain,
    state,
    out_weight,
    hidden,
    post_gain,
    expert_in,
    expert_out,
    expert_ids,
    route_weights,
):
    requests, positions, width = hidden.shape
    row_count = requests * positions
    gated_out = recur(
        query, key_in, value, gate_z, alpha_in, beta_in, a_log, dt_bias, norm_gain, state
    )
    partial_value = jnp.dot(gated_out, out_weight, preferred_element_type=jnp.float32)
    ids_flat = expert_ids.reshape(row_count, -1)
    weights_flat = route_weights.reshape(row_count, -1)
    req_count = lax.axis_size("req")
    ep_count = lax.axis_size("ep")
    ep_index = lax.axis_index("ep")
    per_device = expert_in.shape[0]
    slice_width = width // ep_count
    residual = hidden.reshape(row_count, width).astype(jnp.float32)
    projected_sum = lax.psum(partial_value.astype(jnp.bfloat16), "ep").astype(jnp.float32)
    after_mixer = residual + projected_sum
    normed = (
        after_mixer
        * lax.rsqrt(jnp.mean(after_mixer * after_mixer, axis=1, keepdims=True) + 1e-06)
        * post_gain
    ).astype(jnp.bfloat16)
    mixer_share = lax.dynamic_slice_in_dim(after_mixer, ep_index * slice_width, slice_width, 1)
    groups = lax.broadcasted_iota(jnp.int32, (req_count, per_device), 0)
    halves = lax.broadcasted_iota(jnp.int32, (req_count, per_device), 1)
    targets = (((groups * ep_count + ep_index) * per_device + halves) // 2).reshape(-1)
    placed, picked = route_tables(ids_flat, weights_flat, targets)
    outgoing = jnp.einsum(
        "ndc,nf->dcf", placed.astype(jnp.bfloat16), normed, preferred_element_type=jnp.float32
    )
    outgoing = outgoing.astype(jnp.bfloat16).reshape(req_count, per_device, MOST, width)
    served = run_experts(
        lax.all_to_all(outgoing, "req", split_axis=0, concat_axis=0, tiled=True),
        expert_in,
        expert_out,
    )
    returned = lax.all_to_all(served, "req", split_axis=0, concat_axis=0, tiled=True)
    combine_weights = (placed * picked[:, :, None]).astype(jnp.bfloat16).reshape(row_count, -1)
    expert_rows = jnp.dot(
        combine_weights, returned.reshape(-1, width), preferred_element_type=jnp.float32
    )
    expert_share = lax.psum_scatter(
        expert_rows.astype(jnp.bfloat16), "ep", scatter_dimension=1, tiled=True
    ).astype(jnp.float32)
    mixed = (mixer_share + expert_share).astype(jnp.bfloat16)
    return mixed.reshape(requests, positions, slice_width)


MESH = pl.DeviceIdType.MESH
VMEM_LIMIT = 58 * 1024 * 1024


def mixer_kernel(q_ref, k_ref, v_ref, z_ref, alpha_ref, beta_ref, log_ref, bias_ref, gain_ref, state_ref, weight_ref, out_ref, rows, reads, total, turned):
    head = pl.program_id(0)
    requests = q_ref.shape[0]
    rows[:, 0:2, :] = k_ref[...].astype(jnp.float32)
    rows[:, 2:4, :] = q_ref[...].astype(jnp.float32)
    rows[:, 4:6, :] = v_ref[...].astype(jnp.float32)
    rows[:, 6:8, :] = z_ref[...].astype(jnp.float32)
    reads[...] = lax.dot_general(
        rows[...].astype(jnp.bfloat16),
        state_ref[...].reshape(requests, state_ref.shape[2], state_ref.shape[3]),
        (((2,), (1,)), ((0,), (0,))),
        preferred_element_type=jnp.float32,
    )
    key0, key1, query0, query1 = (rows[:, i, :] for i in range(4))
    value0, value1, gate0, gate1 = (rows[:, i, :] for i in range(4, 8))

    def dot(a, b):
        return jnp.sum(a * b, axis=-1, keepdims=True)

    scale = q_ref.shape[2] ** (-0.5)
    kn0 = lax.rsqrt(dot(key0, key0) + 1e-06)
    kn1 = lax.rsqrt(dot(key1, key1) + 1e-06)
    qn0 = lax.rsqrt(dot(query0, query0) + 1e-06) * scale
    qn1 = lax.rsqrt(dot(query1, query1) + 1e-06) * scale

    heads = alpha_ref.shape[1]

    @pl.when(head == 0)
    def _():
        turned[...] = jnp.zeros_like(turned)
        for t in range(2):
            turned[8 * t : 8 * t + heads, 0:requests] = alpha_ref[t]
            turned[8 * t + 16 : 8 * t + 16 + heads, 0:requests] = beta_ref[t]
        turned[...] = turned[...].T

    def lane_of(values, at):
        lane = lax.broadcasted_iota(jnp.int32, values.shape, 1)
        return jnp.sum(jnp.where(lane == at, values, 0.0), axis=1, keepdims=True)

    rates = turned[0:requests, :]
    decay_scale = -jnp.exp(lane_of(log_ref[...], head))
    bias = lane_of(bias_ref[...], head)
    decay0, decay1 = (
        jnp.exp(decay_scale * jax.nn.softplus(lane_of(rates, head + 8 * t) + bias)) for t in range(2)
    )
    write0, write1 = (jax.nn.sigmoid(lane_of(rates, head + 8 * t + 16)) for t in range(2))
    change0 = (value0 - (decay0 * kn0) * reads[:, 0, :]) * write0
    head0 = (decay0 * qn0) * reads[:, 2, :] + (dot(query0, key0) * qn0 * kn0) * change0
    both = decay0 * decay1
    recalled1 = (both * kn1) * reads[:, 1, :] + (decay1 * dot(key1, key0) * kn1 * kn0) * change0
    change1 = (value1 - recalled1) * write1
    head1 = (
        (both * qn1) * reads[:, 3, :]
        + (decay1 * dot(query1, key0) * qn1 * kn0) * change0
        + (dot(query1, key1) * qn1 * kn1) * change1
    )
    gain = gain_ref[...]

    def finish(out, gate):
        mean = jnp.mean(out * out, axis=-1, keepdims=True)
        return out * lax.rsqrt(mean + 1e-06) * gain * (gate * jax.nn.sigmoid(gate))

    gated = jnp.concatenate([finish(head0, gate0), finish(head1, gate1)], axis=0).astype(jnp.bfloat16)
    part = jnp.dot(gated, weight_ref[...], preferred_element_type=jnp.float32)

    @pl.when(head == 0)
    def _():
        total[...] = part

    @pl.when(head > 0)
    def _():
        total[...] += part

    @pl.when(head == pl.num_programs(0) - 1)
    def _():
        slices, _, width = out_ref.shape
        for s in range(slices):
            out_ref[s] = total[:, s * width : (s + 1) * width].astype(jnp.bfloat16)


def mixer(query, key_in, value, gate_z, alpha_in, beta_in, a_log, dt_bias, norm_gain, state, out_weight, slices):
    requests, positions, _ = query.shape
    heads, key_size, value_size = state.shape[1:]
    width = out_weight.shape[1]
    rows = requests * positions
    row_spec = pl.BlockSpec((requests, positions, key_size), lambda h: (0, 0, h))
    return pl.pallas_call(
        mixer_kernel,
        grid=(heads,),
        out_shape=jax.ShapeDtypeStruct((slices, rows, width // slices), jnp.bfloat16),
        in_specs=[
            row_spec,
            row_spec,
            row_spec,
            row_spec,
            pl.BlockSpec((positions, heads, requests), lambda h: (0, 0, 0)),
            pl.BlockSpec((positions, heads, requests), lambda h: (0, 0, 0)),
            pl.BlockSpec((1, heads), lambda h: (0, 0)),
            pl.BlockSpec((1, heads), lambda h: (0, 0)),
            pl.BlockSpec((1, value_size), lambda h: (0, 0)),
            pl.BlockSpec((requests, 1, key_size, value_size), lambda h: (0, h, 0, 0)),
            pl.BlockSpec((value_size, width), lambda h: (h, 0)),
        ],
        out_specs=pl.BlockSpec((slices, rows, width // slices), lambda h: (0, 0, 0)),
        scratch_shapes=[
            pltpu.VMEM((requests, 8, key_size), jnp.float32),
            pltpu.VMEM((requests, 8, value_size), jnp.float32),
            pltpu.VMEM((rows, width), jnp.float32),
            pltpu.VMEM((128, 128), jnp.float32),
        ],
        compiler_params=pltpu.CompilerParams(vmem_limit_bytes=VMEM_LIMIT),
        name="mixer",
    )(
        query, key_in, value, gate_z, alpha_in.transpose(1, 2, 0), beta_in.transpose(1, 2, 0),
        a_log.reshape(1, -1), dt_bias.reshape(1, -1),
        norm_gain.reshape(1, -1), state, out_weight,
    )


def expert_kernel(
    part_ref, hidden_ref, gain_ref, ids_ref, weights_ref, win_hbm, wout_hbm, out_ref,
    paired, listing, named, table_ref,
    win, wout, rs_buf, after, xall, tables, slots, served, combine,
    send_a, recv_a, own, send_b, recv_b, total, send_c, recv_c,
    w_sem, rs_send, rs_recv, tab_send, tab_recv, z_send, z_recv, pl_send, pl_recv,
    fw_send, fw_recv, a_send, a_recv, b_send, b_recv, c_send, c_recv,
):
    z = lax.axis_index("req")
    me = lax.axis_index("ep")
    core = lax.rem(me, 2)
    chip = me // 2
    chip_x = lax.rem(chip, 2)
    chip_y = chip // 2
    experts = win.shape[0] // 2
    rows, width = after.shape

    def chip_at(m):
        return lax.rem(chip_y + m // 2, 2) * 2 + lax.rem(chip_x + m % 2, 2)

    def mate(m):
        return chip_at(m // 2) * 2 + lax.rem(core + m % 2, 2)

    def level(k):
        return lax.rem(z + k, 4)

    def remote(src, dst, send, recv, device):
        return pltpu.make_async_remote_copy(
            src_ref=src, dst_ref=dst, send_sem=send, recv_sem=recv, device_id=device, device_id_type=MESH
        )

    def weight_copies(e):
        pair = pl.ds(2 * e, 2)
        return (
            pltpu.make_async_copy(win_hbm.at[pair], win.at[pair], w_sem.at[0, e]),
            pltpu.make_async_copy(wout_hbm.at[pair], wout.at[pair], w_sem.at[1, e]),
        )

    barrier = pltpu.get_barrier_semaphore()
    for m in range(1, 8):
        pl.semaphore_signal(barrier, inc=1, device_id=(z, mate(m)), device_id_type=MESH)
    for k in range(1, 4):
        pl.semaphore_signal(barrier, inc=1, device_id=(level(k), me), device_id_type=MESH)
    for e in range(experts):
        for copy in weight_copies(e):
            copy.start()
    odd = lax.rem(z, 2)
    top, positions, requests = ids_ref.shape
    lanes = listing.shape[1]
    from_lane = lax.broadcasted_iota(jnp.int32, (lanes, lanes), 0)
    to_lane = lax.broadcasted_iota(jnp.int32, (lanes, lanes), 1)
    for i, ref in enumerate((ids_ref, weights_ref)):
        named[...] = ref[...].astype(jnp.float32)
        placing = jnp.zeros(listing.shape, jnp.float32)
        for t in range(positions):
            listing[...] = jnp.zeros_like(listing)
            listing[0:top, 0:requests] = named[:, t, :]
            move = jnp.where(to_lane == from_lane + odd * rows + t * requests, 1.0, 0.0).astype(jnp.bfloat16)
            placing = placing + jnp.dot(
                listing[...].astype(jnp.bfloat16), move, preferred_element_type=jnp.float32
            )
        table_ref[16 * i : 16 * i + 16, :] = placing
    tables[0] = table_ref[...]
    paired[...] = hidden_ref[:, :, pl.ds(pl.multiple_of(me * width, width), width)].astype(jnp.float32)
    hidden_rows = jnp.concatenate([paired[:, t, :] for t in range(positions)], axis=0)
    pl.semaphore_wait(barrier, 10)
    sent = []

    for m in (6, 7, 2, 3, 4, 5, 1):
        copy = remote(part_ref.at[mate(m)], rs_buf.at[m - 1], rs_send.at[m - 1], rs_recv.at[m - 1], (z, mate(m)))
        copy.start()
        sent.append(copy)
    for k in range(1, 4):
        copy = remote(table_ref, tables.at[k], tab_send.at[k - 1], tab_recv.at[k - 1], (level(k), me))
        copy.start()
        sent.append(copy)
    total_rows = part_ref[me].astype(jnp.float32) + hidden_rows
    for m in (1, 2, 3, 4, 5, 6, 7):
        remote(rs_buf.at[m - 1], rs_buf.at[m - 1], rs_send.at[m - 1], rs_recv.at[m - 1], (z, mate(m))).wait_recv()
        total_rows = total_rows + rs_buf[m - 1].astype(jnp.float32)
    after[...] = total_rows
    xall[0, me] = total_rows.astype(jnp.bfloat16)

    for k in (3, 2, 1):
        copy = remote(xall.at[0, me], xall.at[k, me], z_send.at[k - 1], z_recv.at[k - 1], (level(k), me))
        copy.start()
        sent.append(copy)
    near = (6, 2, 4, 1)
    for k in range(4):
        if k:
            remote(xall.at[k, me], xall.at[k, me], z_send.at[k - 1], z_recv.at[k - 1], (level(k), me)).wait_recv()
        for i, m in enumerate(near):
            copy = remote(xall.at[k, me], xall.at[k, me], pl_send.at[k, i], pl_recv.at[k, i], (z, mate(m)))
            copy.start()
            sent.append(copy)

    for k in range(1, 4):
        remote(tables.at[k], tables.at[k], tab_send.at[k - 1], tab_recv.at[k - 1], (level(k), me)).wait_recv()
    all_rows = 4 * rows
    listed = jnp.concatenate([tables[0] + tables[1], tables[2] + tables[3]], axis=1)
    column = lax.broadcasted_iota(jnp.int32, (1, all_rows), 1) // rows
    group_of = 2 * (column // 2) + lax.rem(column + odd, 2)
    ep_count = xall.shape[1]
    first = ((z * ep_count + me) * experts).astype(jnp.float32)
    names = first + lax.broadcasted_iota(jnp.int32, (experts, all_rows), 0).astype(jnp.float32)
    member = jnp.zeros((experts, all_rows), jnp.float32)
    picked = jnp.zeros((experts, all_rows), jnp.float32)
    for t in range(top):
        hit = listed[t : t + 1, :] == names
        member = member + jnp.where(hit, 1.0, 0.0)
        picked = picked + jnp.where(hit, listed[16 + t : 17 + t, :], 0.0)
    earlier = lax.broadcasted_iota(jnp.int32, (all_rows, all_rows), 0)
    later = lax.broadcasted_iota(jnp.int32, (all_rows, all_rows), 1)
    precedes = jnp.where((earlier < later) & (earlier // rows == later // rows), 1.0, 0.0)
    before = jnp.dot(member.astype(jnp.bfloat16), precedes.astype(jnp.bfloat16), preferred_element_type=jnp.float32)
    code = jnp.where(member > 0.5, before + (MOST * group_of).astype(jnp.float32), -1.0)
    spots = 4 * MOST
    places = lax.broadcasted_iota(jnp.int32, (experts, spots, all_rows), 1).astype(jnp.float32)
    placed = jnp.where(code[:, None, :] == places, 1.0, 0.0)
    weighted = (placed * picked[:, None, :]).reshape(experts * spots, all_rows)
    placed = placed.reshape(experts * spots, all_rows).astype(jnp.bfloat16)
    combine[...] = weighted.T.astype(jnp.bfloat16)

    for k in range(4):
        for i in range(3):
            other = mate(near[i])
            remote(xall.at[k, other], xall.at[k, other], pl_send.at[k, i], pl_recv.at[k, i], (z, other)).wait_recv()
            copy = remote(xall.at[k, other], xall.at[k, other], fw_send.at[k, i], fw_recv.at[k, i], (z, mate(1)))
            copy.start()
            sent.append(copy)
    for k in range(4):
        remote(xall.at[k, mate(1)], xall.at[k, mate(1)], pl_send.at[k, 3], pl_recv.at[k, 3], (z, mate(1))).wait_recv()
        for i in range(3):
            other = mate(near[i] + 1)
            remote(xall.at[k, other], xall.at[k, other], fw_send.at[k, i], fw_recv.at[k, i], (z, mate(1))).wait_recv()

    squares = jnp.zeros((experts * spots, 1), jnp.float32)
    raw = []
    for s in range(ep_count):
        first_pair = jnp.concatenate([xall[odd, s], xall[1 - odd, s]], axis=0)
        second_pair = jnp.concatenate([xall[2 + odd, s], xall[3 - odd, s]], axis=0)
        block = jnp.concatenate([first_pair, second_pair], axis=0)
        picked_rows = jnp.dot(placed, block, preferred_element_type=jnp.float32)
        squares = squares + jnp.sum(picked_rows * picked_rows, axis=1, keepdims=True)
        slots[:, :, s * width : (s + 1) * width] = picked_rows.astype(jnp.bfloat16).reshape(experts, spots, width)
    unit = lax.rsqrt(squares * (1.0 / (ep_count * width)) + 1e-06).reshape(experts, spots, 1)
    for s in range(ep_count):
        part = slots[:, :, s * width : (s + 1) * width].astype(jnp.float32)
        gain = gain_ref[:, s * width : (s + 1) * width].reshape(1, 1, width)
        slots[:, :, s * width : (s + 1) * width] = (part * unit * gain).astype(jnp.bfloat16)

    half = wout.shape[1]

    def one_expert(e, carry):
        for copy in weight_copies(e):
            copy.wait()
        x = slots[e]
        sums = None
        for j in range(2):
            proj = jnp.dot(x, win[2 * e + j], preferred_element_type=jnp.float32)
            gate = proj[:, :half]
            inner = (gate * jax.nn.sigmoid(gate) * proj[:, half:]).astype(jnp.bfloat16)
            term = jnp.dot(inner, wout[2 * e + j], preferred_element_type=jnp.float32)
            sums = term if sums is None else sums + term
        served[e] = sums.astype(jnp.bfloat16)
        return carry

    lax.fori_loop(0, experts, one_expert, 0)

    def weigh(column_slice):
        block = served[:, :, pl.ds(pl.multiple_of(column_slice * width, width), width)]
        return jnp.dot(
            combine[...], block.reshape(experts * spots, width), preferred_element_type=jnp.float32
        )

    def span_of(k):
        return pl.ds(pl.multiple_of((2 * (k // 2) + lax.rem(k + odd, 2)) * rows, rows), rows)

    order = (3, 1, 2, 0)
    for c in order:
        send_a[c] = weigh(chip_at(c) * 2 + 1 - core).astype(jnp.bfloat16)
        copy = remote(send_a.at[c], recv_a.at[c], a_send.at[c], a_recv.at[c], (z, mate(1)))
        copy.start()
        sent.append(copy)
    for c in order:
        own[c] = weigh(chip_at(c) * 2 + core)
    for c in order:
        remote(recv_a.at[c], recv_a.at[c], a_send.at[c], a_recv.at[c], (z, mate(1))).wait_recv()
        both = own[c] + recv_a[c].astype(jnp.float32)
        if c == 0:
            total[...] = both
        else:
            send_b[c - 1] = both.astype(jnp.bfloat16)
            for k in (3, 2, 1, 0):
                copy = remote(
                    send_b.at[c - 1, span_of(k)], recv_b.at[c - 1, span_of(k)],
                    b_send.at[c - 1, k], b_recv.at[c - 1, k], (z, mate(2 * c)),
                )
                copy.start()
                sent.append(copy)
    for k in (3, 2, 1, 0):
        sums = total[span_of(k), :]
        for c in (1, 2, 3):
            remote(
                recv_b.at[c - 1, span_of(k)], recv_b.at[c - 1, span_of(k)],
                b_send.at[c - 1, k], b_recv.at[c - 1, k], (z, mate(2 * c)),
            ).wait_recv()
            sums = sums + recv_b[c - 1, span_of(k), :].astype(jnp.float32)
        if k:
            send_c[k - 1] = sums.astype(jnp.bfloat16)
            copy = remote(
                send_c.at[k - 1], recv_c.at[k - 1], c_send.at[k - 1], c_recv.at[k - 1], (level(4 - k), me)
            )
            copy.start()
            sent.append(copy)
        else:
            result = after[...] + sums
    for k in (1, 2, 3):
        remote(
            recv_c.at[k - 1], recv_c.at[k - 1], c_send.at[k - 1], c_recv.at[k - 1], (level(k), me)
        ).wait_recv()
        result = result + recv_c[k - 1].astype(jnp.float32)
    for t in range(positions):
        paired[:, t, :] = result[t * requests : (t + 1) * requests]
    out_ref[...] = paired[...].astype(jnp.bfloat16)
    for copy in sent:
        copy.wait_send()


def serve(part, hidden, post_gain, expert_ids, route_weights, expert_in, expert_out):
    slices, rows, width = part.shape
    requests, positions, _ = hidden.shape
    halves, features, columns = expert_in.shape
    half = expert_out.shape[1]
    experts = halves // 2
    spots = 4 * MOST
    bf16, f32 = jnp.bfloat16, jnp.float32
    vmem, dma = pltpu.VMEM, pltpu.SemaphoreType.DMA
    in_vmem = pl.BlockSpec(memory_space=pltpu.VMEM)
    in_hbm = pl.BlockSpec(memory_space=pl.ANY)
    return pl.pallas_call(
        expert_kernel,
        out_shape=jax.ShapeDtypeStruct((requests, positions, width), bf16),
        in_specs=[in_vmem] * 5 + [in_hbm] * 2,
        out_specs=in_vmem,
        scratch_shapes=[
            vmem((requests, positions, width), f32),
            vmem((16, 2 * rows), f32),
            vmem(expert_ids.shape[::-1], f32),
            vmem((32, 2 * rows), f32),
            vmem((halves, features, columns), bf16),
            vmem((halves, half, features), bf16),
            vmem((slices - 1, rows, width), bf16),
            vmem((rows, width), f32),
            vmem((4, slices, rows, width), bf16),
            vmem((4, 32, 2 * rows), f32),
            vmem((experts, spots, features), bf16),
            vmem((experts, spots, features), bf16),
            vmem((4 * rows, experts * spots), bf16),
            vmem((4, 4 * rows, width), bf16),
            vmem((4, 4 * rows, width), bf16),
            vmem((4, 4 * rows, width), f32),
            vmem((3, 4 * rows, width), bf16),
            vmem((3, 4 * rows, width), bf16),
            vmem((4 * rows, width), f32),
            vmem((3, rows, width), bf16),
            vmem((3, rows, width), bf16),
            dma((2, experts)),
            dma((7,)), dma((7,)),
            dma((3,)), dma((3,)),
            dma((3,)), dma((3,)),
            dma((4, 4)), dma((4, 4)),
            dma((4, 3)), dma((4, 3)),
            dma((4,)), dma((4,)),
            dma((3, 4)), dma((3, 4)),
            dma((3,)), dma((3,)),
        ],
        compiler_params=pltpu.CompilerParams(
            collective_id=0, has_side_effects=True, vmem_limit_bytes=VMEM_LIMIT
        ),
        name="experts",
    )(
        part, hidden, post_gain.reshape(1, -1), expert_ids.transpose(2, 1, 0), route_weights.transpose(2, 1, 0),
        expert_in, expert_out,
    )


def in_kernels(
    query, key_in, value, gate_z, alpha_in, beta_in, a_log, dt_bias, norm_gain, state,
    out_weight, hidden, post_gain, expert_in, expert_out, expert_ids, route_weights,
):
    ep_count = lax.axis_size("ep")
    part = mixer(
        query, key_in, value, gate_z, alpha_in, beta_in, a_log, dt_bias, norm_gain, state, out_weight, ep_count
    )
    return serve(part, hidden, post_gain, expert_ids, route_weights, expert_in, expert_out)


def solution(mesh):
    body = in_kernels if mesh.shape["req"] == 4 and mesh.shape["ep"] == 8 else on_device
    return jax.shard_map(
        body,
        mesh=mesh,
        in_specs=(
            P("req", None, "ep"),
            P("req", None, "ep"),
            P("req", None, "ep"),
            P("req", None, "ep"),
            P("req", None, "ep"),
            P("req", None, "ep"),
            P("ep"),
            P("ep"),
            P(),
            P("req", "ep", None, None),
            P("ep", None),
            P("req", None, None),
            P(),
            P(("req", "ep"), None, None),
            P(("req", "ep"), None, None),
            P("req", None, None),
            P("req", None, None),
        ),
        out_specs=P("req", None, "ep"),
        check_vma=False,
    )
```

```python
import jax
import jax.numpy as jnp
from jax import lax
from jax.experimental import pallas as pl
from jax.experimental.pallas import tpu as pltpu
from jax.sharding import PartitionSpec as P

MOST = 4


def unit_rows(values):
    return values * lax.rsqrt(jnp.sum(values * values, axis=-1, keepdims=True) + 1e-06)


def recur(query, key_in, value, gate_z, alpha_in, beta_in, a_log, dt_bias, norm_gain, state):
    requests, positions, head_count = alpha_in.shape
    key_size = state.shape[2]
    value_size = state.shape[3]
    queries = query.astype(jnp.float32).reshape(requests, positions, head_count, key_size)
    key_rows = key_in.astype(jnp.float32).reshape(requests, positions, head_count, key_size)
    value_rows = value.astype(jnp.float32).reshape(requests, positions, head_count, value_size)
    memory = state.astype(jnp.float32)
    decay_scale = -jnp.exp(a_log)
    outputs = []
    for position in range(positions):
        query_unit = unit_rows(queries[:, position]) * key_size ** (-0.5)
        key_unit = unit_rows(key_rows[:, position])
        decay_rate = jnp.exp(decay_scale * jax.nn.softplus(alpha_in[:, position] + dt_bias))
        write_rate = jax.nn.sigmoid(beta_in[:, position])
        memory = memory * decay_rate[:, :, None, None]
        recalled = jnp.einsum("rhk,rhkv->rhv", key_unit, memory, precision=lax.Precision.HIGHEST)
        correction = (value_rows[:, position] - recalled) * write_rate[:, :, None]
        memory = memory + key_unit[:, :, :, None] * correction[:, :, None, :]
        outputs.append(
            jnp.einsum("rhk,rhkv->rhv", query_unit, memory, precision=lax.Precision.HIGHEST)
        )
    head_out = jnp.stack(outputs, axis=1)
    scaled = (
        head_out
        * lax.rsqrt(jnp.mean(head_out * head_out, axis=-1, keepdims=True) + 1e-06)
        * norm_gain
    )
    gate_rows = gate_z.astype(jnp.float32).reshape(requests, positions, head_count, value_size)
    gated_out = (scaled * jax.nn.silu(gate_rows)).astype(jnp.bfloat16)
    return gated_out.reshape(requests * positions, head_count * value_size)


def route_tables(ids_flat, weights_flat, targets):
    hits = ids_flat[:, :, None] == targets[None, None, :]
    member = jnp.any(hits, axis=1).astype(jnp.int32)
    picked = jnp.sum(jnp.where(hits, weights_flat.astype(jnp.float32)[:, :, None], 0.0), axis=1)
    before = jnp.cumsum(member, axis=0) - member
    slot_ids = lax.broadcasted_iota(jnp.int32, (1, 1, MOST), 2)
    placed = (member[:, :, None] == 1) & (before[:, :, None] == slot_ids)
    return (placed, picked)


def run_experts(received, expert_in, expert_out):
    projected = jnp.einsum(
        "rjcd,jdf->rjcf", received, expert_in, preferred_element_type=jnp.float32
    )
    half_units = expert_out.shape[1]
    inner = (jax.nn.silu(projected[..., :half_units]) * projected[..., half_units:]).astype(
        jnp.bfloat16
    )
    return jnp.einsum(
        "rjch,jhd->rjcd", inner, expert_out, preferred_element_type=jnp.float32
    ).astype(jnp.bfloat16)


def on_device(
    query,
    key_in,
    value,
    gate_z,
    alpha_in,
    beta_in,
    a_log,
    dt_bias,
    norm_gain,
    state,
    out_weight,
    hidden,
    post_gain,
    expert_in,
    expert_out,
    expert_ids,
    route_weights,
):
    requests, positions, width = hidden.shape
    row_count = requests * positions
    gated_out = recur(
        query, key_in, value, gate_z, alpha_in, beta_in, a_log, dt_bias, norm_gain, state
    )
    partial_value = jnp.dot(gated_out, out_weight, preferred_element_type=jnp.float32)
    ids_flat = expert_ids.reshape(row_count, -1)
    weights_flat = route_weights.reshape(row_count, -1)
    req_count = lax.axis_size("req")
    ep_count = lax.axis_size("ep")
    ep_index = lax.axis_index("ep")
    per_device = expert_in.shape[0]
    slice_width = width // ep_count
    residual = hidden.reshape(row_count, width).astype(jnp.float32)
    projected_sum = lax.psum(partial_value.astype(jnp.bfloat16), "ep").astype(jnp.float32)
    after_mixer = residual + projected_sum
    normed = (
        after_mixer
        * lax.rsqrt(jnp.mean(after_mixer * after_mixer, axis=1, keepdims=True) + 1e-06)
        * post_gain
    ).astype(jnp.bfloat16)
    mixer_share = lax.dynamic_slice_in_dim(after_mixer, ep_index * slice_width, slice_width, 1)
    groups = lax.broadcasted_iota(jnp.int32, (req_count, per_device), 0)
    halves = lax.broadcasted_iota(jnp.int32, (req_count, per_device), 1)
    targets = (((groups * ep_count + ep_index) * per_device + halves) // 2).reshape(-1)
    placed, picked = route_tables(ids_flat, weights_flat, targets)
    outgoing = jnp.einsum(
        "ndc,nf->dcf", placed.astype(jnp.bfloat16), normed, preferred_element_type=jnp.float32
    )
    outgoing = outgoing.astype(jnp.bfloat16).reshape(req_count, per_device, MOST, width)
    served = run_experts(
        lax.all_to_all(outgoing, "req", split_axis=0, concat_axis=0, tiled=True),
        expert_in,
        expert_out,
    )
    returned = lax.all_to_all(served, "req", split_axis=0, concat_axis=0, tiled=True)
    combine_weights = (placed * picked[:, :, None]).astype(jnp.bfloat16).reshape(row_count, -1)
    expert_rows = jnp.dot(
        combine_weights, returned.reshape(-1, width), preferred_element_type=jnp.float32
    )
    expert_share = lax.psum_scatter(
        expert_rows.astype(jnp.bfloat16), "ep", scatter_dimension=1, tiled=True
    ).astype(jnp.float32)
    mixed = (mixer_share + expert_share).astype(jnp.bfloat16)
    return mixed.reshape(requests, positions, slice_width)


MESH = pl.DeviceIdType.MESH
VMEM_LIMIT = 58 * 1024 * 1024


def mixer_kernel(q_ref, k_ref, v_ref, z_ref, alpha_ref, beta_ref, log_ref, bias_ref, gain_ref, state_ref, weight_ref, out_ref, rows, reads, total, turned):
    head = pl.program_id(0)
    requests = q_ref.shape[0]
    rows[:, 0:2, :] = k_ref[...].astype(jnp.float32)
    rows[:, 2:4, :] = q_ref[...].astype(jnp.float32)
    rows[:, 4:6, :] = v_ref[...].astype(jnp.float32)
    rows[:, 6:8, :] = z_ref[...].astype(jnp.float32)
    reads[...] = lax.dot_general(
        rows[...].astype(jnp.bfloat16),
        state_ref[...].reshape(requests, state_ref.shape[2], state_ref.shape[3]),
        (((2,), (1,)), ((0,), (0,))),
        preferred_element_type=jnp.float32,
    )
    key0, key1, query0, query1 = (rows[:, i, :] for i in range(4))
    value0, value1, gate0, gate1 = (rows[:, i, :] for i in range(4, 8))

    def dot(a, b):
        return jnp.sum(a * b, axis=-1, keepdims=True)

    scale = q_ref.shape[2] ** (-0.5)
    kn0 = lax.rsqrt(dot(key0, key0) + 1e-06)
    kn1 = lax.rsqrt(dot(key1, key1) + 1e-06)
    qn0 = lax.rsqrt(dot(query0, query0) + 1e-06) * scale
    qn1 = lax.rsqrt(dot(query1, query1) + 1e-06) * scale

    heads = alpha_ref.shape[1]

    @pl.when(head == 0)
    def _():
        turned[...] = jnp.zeros_like(turned)
        for t in range(2):
            turned[8 * t : 8 * t + heads, 0:requests] = alpha_ref[t]
            turned[8 * t + 16 : 8 * t + 16 + heads, 0:requests] = beta_ref[t]
        turned[...] = turned[...].T

    def lane_of(values, at):
        lane = lax.broadcasted_iota(jnp.int32, values.shape, 1)
        return jnp.sum(jnp.where(lane == at, values, 0.0), axis=1, keepdims=True)

    rates = turned[0:requests, :]
    decay_scale = -jnp.exp(lane_of(log_ref[...], head))
    bias = lane_of(bias_ref[...], head)
    decay0, decay1 = (
        jnp.exp(decay_scale * jax.nn.softplus(lane_of(rates, head + 8 * t) + bias)) for t in range(2)
    )
    write0, write1 = (jax.nn.sigmoid(lane_of(rates, head + 8 * t + 16)) for t in range(2))
    change0 = (value0 - (decay0 * kn0) * reads[:, 0, :]) * write0
    head0 = (decay0 * qn0) * reads[:, 2, :] + (dot(query0, key0) * qn0 * kn0) * change0
    both = decay0 * decay1
    recalled1 = (both * kn1) * reads[:, 1, :] + (decay1 * dot(key1, key0) * kn1 * kn0) * change0
    change1 = (value1 - recalled1) * write1
    head1 = (
        (both * qn1) * reads[:, 3, :]
        + (decay1 * dot(query1, key0) * qn1 * kn0) * change0
        + (dot(query1, key1) * qn1 * kn1) * change1
    )
    gain = gain_ref[...]

    def finish(out, gate):
        mean = jnp.mean(out * out, axis=-1, keepdims=True)
        return out * lax.rsqrt(mean + 1e-06) * gain * (gate * jax.nn.sigmoid(gate))

    gated = jnp.concatenate([finish(head0, gate0), finish(head1, gate1)], axis=0).astype(jnp.bfloat16)
    part = jnp.dot(gated, weight_ref[...], preferred_element_type=jnp.float32)

    @pl.when(head == 0)
    def _():
        total[...] = part

    @pl.when(head > 0)
    def _():
        total[...] += part

    @pl.when(head == pl.num_programs(0) - 1)
    def _():
        slices, _, width = out_ref.shape
        for s in range(slices):
            out_ref[s] = total[:, s * width : (s + 1) * width].astype(jnp.bfloat16)


def mixer(query, key_in, value, gate_z, alpha_in, beta_in, a_log, dt_bias, norm_gain, state, out_weight, slices):
    requests, positions, _ = query.shape
    heads, key_size, value_size = state.shape[1:]
    width = out_weight.shape[1]
    rows = requests * positions
    row_spec = pl.BlockSpec((requests, positions, key_size), lambda h: (0, 0, h))
    return pl.pallas_call(
        mixer_kernel,
        grid=(heads,),
        out_shape=jax.ShapeDtypeStruct((slices, rows, width // slices), jnp.bfloat16),
        in_specs=[
            row_spec,
            row_spec,
            row_spec,
            row_spec,
            pl.BlockSpec((positions, heads, requests), lambda h: (0, 0, 0)),
            pl.BlockSpec((positions, heads, requests), lambda h: (0, 0, 0)),
            pl.BlockSpec((1, heads), lambda h: (0, 0)),
            pl.BlockSpec((1, heads), lambda h: (0, 0)),
            pl.BlockSpec((1, value_size), lambda h: (0, 0)),
            pl.BlockSpec((requests, 1, key_size, value_size), lambda h: (0, h, 0, 0)),
            pl.BlockSpec((value_size, width), lambda h: (h, 0)),
        ],
        out_specs=pl.BlockSpec((slices, rows, width // slices), lambda h: (0, 0, 0)),
        scratch_shapes=[
            pltpu.VMEM((requests, 8, key_size), jnp.float32),
            pltpu.VMEM((requests, 8, value_size), jnp.float32),
            pltpu.VMEM((rows, width), jnp.float32),
            pltpu.VMEM((128, 128), jnp.float32),
        ],
        compiler_params=pltpu.CompilerParams(vmem_limit_bytes=VMEM_LIMIT),
        name="mixer",
    )(
        query, key_in, value, gate_z, alpha_in.transpose(1, 2, 0), beta_in.transpose(1, 2, 0),
        a_log.reshape(1, -1), dt_bias.reshape(1, -1),
        norm_gain.reshape(1, -1), state, out_weight,
    )


def expert_kernel(
    part_ref, hidden_ref, gain_ref, ids_ref, weights_ref, win_hbm, wout_hbm, out_ref,
    paired, listing, named, table_ref,
    win, wout, rs_buf, after, xall, tables, slots, served, combine,
    send_a, recv_a, own, send_b, recv_b, total, send_c, recv_c,
    w_sem, rs_send, rs_recv, tab_send, tab_recv, z_send, z_recv, pl_send, pl_recv,
    fw_send, fw_recv, pt_send, pt_recv, a_send, a_recv, b_send, b_recv, c_send, c_recv,
):
    z = lax.axis_index("req")
    me = lax.axis_index("ep")
    core = lax.rem(me, 2)
    chip = me // 2
    chip_x = lax.rem(chip, 2)
    chip_y = chip // 2
    experts = win.shape[0] // 2
    rows, width = after.shape

    def chip_at(m):
        return lax.rem(chip_y + m // 2, 2) * 2 + lax.rem(chip_x + m % 2, 2)

    def mate(m):
        return chip_at(m // 2) * 2 + lax.rem(core + m % 2, 2)

    def level(k):
        return lax.rem(z + k, 4)

    def remote(src, dst, send, recv, device):
        return pltpu.make_async_remote_copy(
            src_ref=src, dst_ref=dst, send_sem=send, recv_sem=recv, device_id=device, device_id_type=MESH
        )

    def weight_copies(e):
        pair = pl.ds(2 * e, 2)
        return (
            pltpu.make_async_copy(win_hbm.at[pair], win.at[pair], w_sem.at[0, e]),
            pltpu.make_async_copy(wout_hbm.at[pair], wout.at[pair], w_sem.at[1, e]),
        )

    barrier = pltpu.get_barrier_semaphore()
    for m in range(1, 8):
        pl.semaphore_signal(barrier, inc=1, device_id=(z, mate(m)), device_id_type=MESH)
    for k in range(1, 4):
        pl.semaphore_signal(barrier, inc=1, device_id=(level(k), me), device_id_type=MESH)
    for e in range(experts):
        for copy in weight_copies(e):
            copy.start()
    odd = lax.rem(z, 2)
    top, positions, requests = ids_ref.shape
    lanes = listing.shape[1]
    from_lane = lax.broadcasted_iota(jnp.int32, (lanes, lanes), 0)
    to_lane = lax.broadcasted_iota(jnp.int32, (lanes, lanes), 1)
    for i, ref in enumerate((ids_ref, weights_ref)):
        named[...] = ref[...].astype(jnp.float32)
        placing = jnp.zeros(listing.shape, jnp.float32)
        for t in range(positions):
            listing[...] = jnp.zeros_like(listing)
            listing[0:top, 0:requests] = named[:, t, :]
            move = jnp.where(to_lane == from_lane + odd * rows + t * requests, 1.0, 0.0).astype(jnp.bfloat16)
            placing = placing + jnp.dot(
                listing[...].astype(jnp.bfloat16), move, preferred_element_type=jnp.float32
            )
        table_ref[16 * i : 16 * i + 16, :] = placing
    tables[0] = table_ref[...]
    paired[...] = hidden_ref[:, :, pl.ds(pl.multiple_of(me * width, width), width)].astype(jnp.float32)
    hidden_rows = jnp.concatenate([paired[:, t, :] for t in range(positions)], axis=0)
    pl.semaphore_wait(barrier, 10)
    sent = []

    for m in (6, 7, 2, 3, 4, 5, 1):
        copy = remote(part_ref.at[mate(m)], rs_buf.at[m - 1], rs_send.at[m - 1], rs_recv.at[m - 1], (z, mate(m)))
        copy.start()
        sent.append(copy)
    for k in range(1, 4):
        copy = remote(table_ref, tables.at[k], tab_send.at[k - 1], tab_recv.at[k - 1], (level(k), me))
        copy.start()
        sent.append(copy)
    total_rows = part_ref[me].astype(jnp.float32) + hidden_rows
    for m in (1, 2, 3, 4, 5, 6, 7):
        remote(rs_buf.at[m - 1], rs_buf.at[m - 1], rs_send.at[m - 1], rs_recv.at[m - 1], (z, mate(m))).wait_recv()
        total_rows = total_rows + rs_buf[m - 1].astype(jnp.float32)
    after[...] = total_rows
    xall[0, me] = total_rows.astype(jnp.bfloat16)

    for k in (3, 2, 1):
        copy = remote(xall.at[0, me], xall.at[k, me], z_send.at[k - 1], z_recv.at[k - 1], (level(k), me))
        copy.start()
        sent.append(copy)
    near = (6, 2, 4, 1)
    from_pair, to_pair = 3 - 2 * odd, 1 + 2 * odd

    def arrived(k):
        remote(xall.at[k, me], xall.at[k, me], z_send.at[k - 1], z_recv.at[k - 1], (level(k), me)).wait_recv()

    def spread(k, choice):
        for i in choice:
            copy = remote(xall.at[k, me], xall.at[k, me], pl_send.at[k, i], pl_recv.at[k, i], (z, mate(near[i])))
            copy.start()
            sent.append(copy)

    spread(0, (0, 1, 2, 3))
    arrived(to_pair)
    spread(to_pair, (0, 1, 2, 3))
    arrived(2)
    spread(2, (0, 1, 2, 3))
    arrived(from_pair)
    spread(from_pair, (3,))

    for k in range(1, 4):
        remote(tables.at[k], tables.at[k], tab_send.at[k - 1], tab_recv.at[k - 1], (level(k), me)).wait_recv()
    all_rows = 4 * rows
    listed = jnp.concatenate([tables[0] + tables[1], tables[2] + tables[3]], axis=1)
    column = lax.broadcasted_iota(jnp.int32, (1, all_rows), 1) // rows
    group_of = 2 * (column // 2) + lax.rem(column + odd, 2)
    ep_count = xall.shape[1]
    first = ((z * ep_count + me) * experts).astype(jnp.float32)
    names = first + lax.broadcasted_iota(jnp.int32, (experts, all_rows), 0).astype(jnp.float32)
    member = jnp.zeros((experts, all_rows), jnp.float32)
    picked = jnp.zeros((experts, all_rows), jnp.float32)
    for t in range(top):
        hit = listed[t : t + 1, :] == names
        member = member + jnp.where(hit, 1.0, 0.0)
        picked = picked + jnp.where(hit, listed[16 + t : 17 + t, :], 0.0)
    earlier = lax.broadcasted_iota(jnp.int32, (all_rows, all_rows), 0)
    later = lax.broadcasted_iota(jnp.int32, (all_rows, all_rows), 1)
    precedes = jnp.where((earlier < later) & (earlier // rows == later // rows), 1.0, 0.0)
    before = jnp.dot(member.astype(jnp.bfloat16), precedes.astype(jnp.bfloat16), preferred_element_type=jnp.float32)
    code = jnp.where(member > 0.5, before + (MOST * group_of).astype(jnp.float32), -1.0)
    spots = 4 * MOST
    places = lax.broadcasted_iota(jnp.int32, (experts, spots, all_rows), 1).astype(jnp.float32)
    placed = jnp.where(code[:, None, :] == places, 1.0, 0.0)
    weighted = (placed * picked[:, None, :]).reshape(experts * spots, all_rows)
    placed = placed.reshape(experts * spots, all_rows).astype(jnp.bfloat16)
    combine[...] = weighted.T.astype(jnp.bfloat16)

    def pass_on(k, i):
        other = mate(near[i])
        copy = remote(xall.at[k, other], xall.at[k, other], fw_send.at[k, i], fw_recv.at[k, i], (z, mate(1)))
        copy.start()
        sent.append(copy)

    for k in (0, to_pair, 2):
        for i in (1, 2, 0):
            other = mate(near[i])
            remote(xall.at[k, other], xall.at[k, other], pl_send.at[k, i], pl_recv.at[k, i], (z, other)).wait_recv()
            if isinstance(k, int) and k == 0:
                copy = remote(
                    xall.at[0, other], xall.at[to_pair, other], pt_send.at[i], pt_recv.at[i],
                    (z + 1 - 2 * odd, me),
                )
                copy.start()
                sent.append(copy)
            pass_on(k, i)
    for i in (1, 2, 0):
        other = mate(near[i])
        remote(
            xall.at[from_pair, other], xall.at[from_pair, other], pt_send.at[i], pt_recv.at[i], (z, mate(1))
        ).wait_recv()
        pass_on(from_pair, i)
    for k in (0, to_pair, 2, from_pair):
        remote(xall.at[k, mate(1)], xall.at[k, mate(1)], pl_send.at[k, 3], pl_recv.at[k, 3], (z, mate(1))).wait_recv()
        for i in range(3):
            other = mate(near[i] + 1)
            remote(xall.at[k, other], xall.at[k, other], fw_send.at[k, i], fw_recv.at[k, i], (z, mate(1))).wait_recv()

    squares = jnp.zeros((experts * spots, 1), jnp.float32)
    raw = []
    for s in range(ep_count):
        first_pair = jnp.concatenate([xall[odd, s], xall[1 - odd, s]], axis=0)
        second_pair = jnp.concatenate([xall[2 + odd, s], xall[3 - odd, s]], axis=0)
        block = jnp.concatenate([first_pair, second_pair], axis=0)
        picked_rows = jnp.dot(placed, block, preferred_element_type=jnp.float32)
        squares = squares + jnp.sum(picked_rows * picked_rows, axis=1, keepdims=True)
        slots[:, :, s * width : (s + 1) * width] = picked_rows.astype(jnp.bfloat16).reshape(experts, spots, width)
    unit = lax.rsqrt(squares * (1.0 / (ep_count * width)) + 1e-06).reshape(experts, spots, 1)
    for s in range(ep_count):
        part = slots[:, :, s * width : (s + 1) * width].astype(jnp.float32)
        gain = gain_ref[:, s * width : (s + 1) * width].reshape(1, 1, width)
        slots[:, :, s * width : (s + 1) * width] = (part * unit * gain).astype(jnp.bfloat16)

    half = wout.shape[1]

    def one_expert(e, carry):
        for copy in weight_copies(e):
            copy.wait()
        x = slots[e]
        sums = None
        for j in range(2):
            proj = jnp.dot(x, win[2 * e + j], preferred_element_type=jnp.float32)
            gate = proj[:, :half]
            inner = (gate * jax.nn.sigmoid(gate) * proj[:, half:]).astype(jnp.bfloat16)
            term = jnp.dot(inner, wout[2 * e + j], preferred_element_type=jnp.float32)
            sums = term if sums is None else sums + term
        served[e] = sums.astype(jnp.bfloat16)
        return carry

    lax.fori_loop(0, experts, one_expert, 0)

    def weigh(column_slice):
        block = served[:, :, pl.ds(pl.multiple_of(column_slice * width, width), width)]
        return jnp.dot(
            combine[...], block.reshape(experts * spots, width), preferred_element_type=jnp.float32
        )

    def span_of(k):
        return pl.ds(pl.multiple_of((2 * (k // 2) + lax.rem(k + odd, 2)) * rows, rows), rows)

    order = (3, 1, 2, 0)
    for c in order:
        send_a[c] = weigh(chip_at(c) * 2 + 1 - core).astype(jnp.bfloat16)
        copy = remote(send_a.at[c], recv_a.at[c], a_send.at[c], a_recv.at[c], (z, mate(1)))
        copy.start()
        sent.append(copy)
    for c in order:
        own[c] = weigh(chip_at(c) * 2 + core)
    for c in order:
        remote(recv_a.at[c], recv_a.at[c], a_send.at[c], a_recv.at[c], (z, mate(1))).wait_recv()
        both = own[c] + recv_a[c].astype(jnp.float32)
        if c == 0:
            total[...] = both
        else:
            send_b[c - 1] = both.astype(jnp.bfloat16)
            for k in (3, 2, 1, 0):
                copy = remote(
                    send_b.at[c - 1, span_of(k)], recv_b.at[c - 1, span_of(k)],
                    b_send.at[c - 1, k], b_recv.at[c - 1, k], (z, mate(2 * c)),
                )
                copy.start()
                sent.append(copy)
    for k in (3, 2, 1, 0):
        sums = total[span_of(k), :]
        for c in (1, 2, 3):
            remote(
                recv_b.at[c - 1, span_of(k)], recv_b.at[c - 1, span_of(k)],
                b_send.at[c - 1, k], b_recv.at[c - 1, k], (z, mate(2 * c)),
            ).wait_recv()
            sums = sums + recv_b[c - 1, span_of(k), :].astype(jnp.float32)
        if k:
            send_c[k - 1] = sums.astype(jnp.bfloat16)
            copy = remote(
                send_c.at[k - 1], recv_c.at[k - 1], c_send.at[k - 1], c_recv.at[k - 1], (level(4 - k), me)
            )
            copy.start()
            sent.append(copy)
        else:
            result = after[...] + sums
    for k in (1, 2, 3):
        remote(
            recv_c.at[k - 1], recv_c.at[k - 1], c_send.at[k - 1], c_recv.at[k - 1], (level(k), me)
        ).wait_recv()
        result = result + recv_c[k - 1].astype(jnp.float32)
    for t in range(positions):
        paired[:, t, :] = result[t * requests : (t + 1) * requests]
    out_ref[...] = paired[...].astype(jnp.bfloat16)
    for copy in sent:
        copy.wait_send()


def serve(part, hidden, post_gain, expert_ids, route_weights, expert_in, expert_out):
    slices, rows, width = part.shape
    requests, positions, _ = hidden.shape
    halves, features, columns = expert_in.shape
    half = expert_out.shape[1]
    experts = halves // 2
    spots = 4 * MOST
    bf16, f32 = jnp.bfloat16, jnp.float32
    vmem, dma = pltpu.VMEM, pltpu.SemaphoreType.DMA
    in_vmem = pl.BlockSpec(memory_space=pltpu.VMEM)
    in_hbm = pl.BlockSpec(memory_space=pl.ANY)
    return pl.pallas_call(
        expert_kernel,
        out_shape=jax.ShapeDtypeStruct((requests, positions, width), bf16),
        in_specs=[in_vmem] * 5 + [in_hbm] * 2,
        out_specs=in_vmem,
        scratch_shapes=[
            vmem((requests, positions, width), f32),
            vmem((16, 2 * rows), f32),
            vmem(expert_ids.shape[::-1], f32),
            vmem((32, 2 * rows), f32),
            vmem((halves, features, columns), bf16),
            vmem((halves, half, features), bf16),
            vmem((slices - 1, rows, width), bf16),
            vmem((rows, width), f32),
            vmem((4, slices, rows, width), bf16),
            vmem((4, 32, 2 * rows), f32),
            vmem((experts, spots, features), bf16),
            vmem((experts, spots, features), bf16),
            vmem((4 * rows, experts * spots), bf16),
            vmem((4, 4 * rows, width), bf16),
            vmem((4, 4 * rows, width), bf16),
            vmem((4, 4 * rows, width), f32),
            vmem((3, 4 * rows, width), bf16),
            vmem((3, 4 * rows, width), bf16),
            vmem((4 * rows, width), f32),
            vmem((3, rows, width), bf16),
            vmem((3, rows, width), bf16),
            dma((2, experts)),
            dma((7,)), dma((7,)),
            dma((3,)), dma((3,)),
            dma((3,)), dma((3,)),
            dma((4, 4)), dma((4, 4)),
            dma((4, 3)), dma((4, 3)),
            dma((3,)), dma((3,)),
            dma((4,)), dma((4,)),
            dma((3, 4)), dma((3, 4)),
            dma((3,)), dma((3,)),
        ],
        compiler_params=pltpu.CompilerParams(
            collective_id=0, has_side_effects=True, vmem_limit_bytes=VMEM_LIMIT
        ),
        name="experts",
    )(
        part, hidden, post_gain.reshape(1, -1), expert_ids.transpose(2, 1, 0), route_weights.transpose(2, 1, 0),
        expert_in, expert_out,
    )


def in_kernels(
    query, key_in, value, gate_z, alpha_in, beta_in, a_log, dt_bias, norm_gain, state,
    out_weight, hidden, post_gain, expert_in, expert_out, expert_ids, route_weights,
):
    ep_count = lax.axis_size("ep")
    part = mixer(
        query, key_in, value, gate_z, alpha_in, beta_in, a_log, dt_bias, norm_gain, state, out_weight, ep_count
    )
    return serve(part, hidden, post_gain, expert_ids, route_weights, expert_in, expert_out)


def solution(mesh):
    body = in_kernels if mesh.shape["req"] == 4 and mesh.shape["ep"] == 8 else on_device
    return jax.shard_map(
        body,
        mesh=mesh,
        in_specs=(
            P("req", None, "ep"),
            P("req", None, "ep"),
            P("req", None, "ep"),
            P("req", None, "ep"),
            P("req", None, "ep"),
            P("req", None, "ep"),
            P("ep"),
            P("ep"),
            P(),
            P("req", "ep", None, None),
            P("ep", None),
            P("req", None, None),
            P(),
            P(("req", "ep"), None, None),
            P(("req", "ep"), None, None),
            P("req", None, None),
            P("req", None, None),
        ),
        out_specs=P("req", None, "ep"),
        check_vma=False,
    )
```
